256 devices in a mesh: dp: 128 (over z, y, x_hi, core), rep: 2 (over x_lo).
Axes of the slice: x: 4 (x_hi: 2, x_lo: 2; x = x_hi * 2 + x_lo), y: 4, z: 8, core: 2. Of those that a mesh axis runs over, the one named last changes fastest.
Arguments:
- images: bfloat16 [2, 32768, 1152], P('rep', 'dp'), may hold values from -6 to 6
- texts: bfloat16 [2, 32768, 1152], P('rep', 'dp'), may hold values from -6 to 6
- img_head: bfloat16 [1152, 1152], replicated, may hold values from -0.1875 to 0.1875
- txt_head: bfloat16 [1152, 1152], replicated, may hold values from -0.1875 to 0.1875
- log_scale: float32 [], replicated, may hold values from 3 to 3.6
- bias: float32 [], replicated, may hold values from -3 to -1
Outputs:
- row_losses: float32 [2, 32768], P('rep', 'dp')
- head_grads: float32 [2304, 1152], P(('dp', 'rep'))
The draws below stay inside these ranges and needn't reach their ends.
All inputs are finite; a program needn't handle non-finite values.
Results may differ from the reference program's by a relative error of at most 0.0025.
Values may be sent and summed in bfloat16 or wider, within the bound.
No kernel may reach another device: no remote copies, remote signals or barrier semaphores. Data moves between devices by JAX's collectives and lax.ppermute only.
A program may use at most 128 MiB of HBM per device.

```python
import jax
import jax.numpy as jnp
from jax import lax

D = 1152
BLOCK = 256
STEPS = 4
ROWS = 32768
N_DP = 128
N_REP = 2


def shard_levels(rng, dims, pieces, low, high):
    def one(dim, shards_of):
        steps = jax.random.uniform(jax.random.fold_in(jax.random.fold_in(rng, 6), dim), (shards_of,), jnp.float32, low / len(pieces), high / len(pieces))
        return jnp.repeat(jnp.exp(steps), dims[dim] // shards_of).reshape((-1,) + (1,) * (len(dims) - dim - 1))

    level = one(*pieces[0])
    for cut in pieces[1:]:
        level = level * one(*cut)
    return level


def centred(stream_key, dims, scale, most, split=(), kind=jnp.bfloat16):
    factor_of = shard_levels(stream_key, dims, split, -0.22, 0.18) if split else 1.0
    result = jax.random.normal(stream_key, dims, jnp.float32) * scale * factor_of
    return jnp.minimum(jnp.maximum(result, -most), most).astype(kind)


def setup_inputs(seed: int = 0) -> dict:
    key_of = jax.random.split(jax.random.key(seed), 7)
    images = centred(key_of[0], (N_REP, ROWS, D), 1.0, 6.0, ((0, 2), (1, 128)))
    texts = centred(key_of[1], (N_REP, ROWS, D), 1.0, 6.0, ((0, 2), (1, 128)))
    img_head = centred(key_of[2], (D, D), D ** -0.5, 0.1875)
    txt_head = centred(key_of[3], (D, D), D ** -0.5, 0.1875)
    log_scale = jnp.clip(jax.random.uniform(key_of[4], (), jnp.float32, 3.0, 3.6), 3.0, 3.6)
    bias = jnp.clip(jax.random.uniform(key_of[5], (), jnp.float32, -3.0, -1.0), -3.0, -1.0)
    return {"images": images, "texts": texts, "img_head": img_head, "txt_head": txt_head, "log_scale": log_scale, "bias": bias}


def normed(feats, head):
    u = jnp.dot(feats, head, preferred_element_type=jnp.float32)
    inv = lax.rsqrt(lax.optimization_barrier(jnp.sum(u * u, axis=-1, keepdims=True)) + 1e-06)
    return (u * inv, inv)

def backnorm(grad, zfull, inv):
    return (inv * (grad - zfull * lax.optimization_barrier(jnp.sum(grad * zfull, axis=-1, keepdims=True)))).astype(jnp.bfloat16)

def reference(images, texts, img_head, txt_head, log_scale, bias):
    scale = jnp.exp(log_scale)
    ident = jnp.eye(BLOCK, dtype=jnp.float32)
    losses = []
    grad_img = jnp.zeros((D, D), jnp.float32)
    grad_txt = jnp.zeros((D, D), jnp.float32)
    for group in range(N_REP):
        zf_img, inv_img = normed(images[group], img_head)
        zf_txt, inv_txt = normed(texts[group], txt_head)
        z_img = zf_img.astype(jnp.bfloat16).reshape(N_DP, BLOCK, D)
        z_txt = zf_txt.astype(jnp.bfloat16).reshape(N_DP, BLOCK, D)
        row_loss = jnp.zeros((N_DP, BLOCK), jnp.float32)
        g_img = jnp.zeros((N_DP, BLOCK, D), jnp.float32)
        g_txt = jnp.zeros((N_DP, BLOCK, D), jnp.float32)
        for step in range(STEPS):
            labels = 2.0 * ident - 1.0 if step == 0 else -jnp.ones_like(ident)
            keys = jnp.roll(z_txt, step, axis=0)

            def tile(pair):
                query, key_block = pair
                logits = scale * jnp.dot(query, key_block.T, preferred_element_type=jnp.float32) + bias
                loss_row = lax.optimization_barrier(jnp.sum(jax.nn.softplus(-labels * logits), axis=1))
                gt_tile = (scale * (-labels * jax.nn.sigmoid(-labels * logits)) / BLOCK).astype(jnp.bfloat16)
                dq = jnp.dot(gt_tile, key_block, preferred_element_type=jnp.float32)
                dk = jnp.dot(gt_tile.T, query, preferred_element_type=jnp.float32)
                return (loss_row, dq, dk)
            loss_row, dq, dk = lax.map(tile, (z_img, keys))
            row_loss = row_loss + loss_row
            g_img = g_img + dq
            g_txt = g_txt + jnp.roll(dk, -step, axis=0)
        losses.append(row_loss.reshape(ROWS))
        du_img = backnorm(g_img.reshape(ROWS, D), zf_img, inv_img)
        du_txt = backnorm(g_txt.reshape(ROWS, D), zf_txt, inv_txt)
        grad_img = grad_img + jnp.dot(images[group].T, du_img, preferred_element_type=jnp.float32)
        grad_txt = grad_txt + jnp.dot(texts[group].T, du_txt, preferred_element_type=jnp.float32)
    return (jnp.stack(losses, axis=0), jnp.concatenate([grad_img, grad_txt], axis=0))
```

```python
import jax
import jax.numpy as jnp
import numpy as np
from jax import lax
from jax.sharding import Mesh, PartitionSpec as P

AXES = ("z", "y", "xh", "c", "xl")
NZ, NY, NX = 8, 4, 4
BLOCK = 256
ROWS9 = 9


def place(i):
    return i // 32, (i // 8) % 4, ((i // 4) % 2) * 2 + i % 2, (i // 2) % 2


def index(z, y, x, c):
    return (((z * NY + y) * 2 + x // 2) * 2 + c) * 2 + x % 2


def chip_shift(by):
    pairs = []
    for i in range(256):
        z, y, x, c = place(i)
        q = (((z * NY + y) * 2 + x // 2) + by) % 64
        pairs.append((i, index(q // 8, (q // 2) % 4, (q % 2) * 2 + x % 2, c)))
    return pairs


def core_swap():
    return [(i, index(*place(i)[:3], 1 - place(i)[3])) for i in range(256)]


def grouped(key, order):
    found = {}
    for i in range(256):
        found.setdefault(key(*place(i)), []).append(i)
    return [sorted(v, key=lambda i: order(*place(i))) for v in found.values()]


def first_groups():
    return grouped(
        lambda z, y, x, c: (c, y, z // 2) if c == 0 else (c, x, ((z + 1) % NZ) // 2),
        lambda z, y, x, c: (z % 2, x if c == 0 else y),
    )


def second_groups():
    return grouped(
        lambda z, y, x, c: (c, x if c == 0 else y, z % 2),
        lambda z, y, x, c: (z // 2, y if c == 0 else x),
    )


def row_order():
    out = np.zeros((2, 2, 576), np.int32)
    for c in range(2):
        for modality in range(2):
            rows = []
            for zl in range(2):
                for a in range(4):
                    for zh in (2 * modality, 2 * modality + 1):
                        for b in range(4):
                            x, y = (a, b) if c == 0 else (b, a)
                            first = 9 * index(2 * zh + zl, y, x, c) - 1152 * modality
                            rows.extend(range(first, first + 9))
            out[c, modality] = rows
    return out


def normed(feats, head):
    u = jnp.dot(feats, head, preferred_element_type=jnp.float32)
    inv = lax.rsqrt(jnp.sum(u * u, axis=-1, keepdims=True) + 1e-06)
    return (u * inv, inv)


def backnorm(grad, zfull, inv):
    return (inv * (grad - zfull * jnp.sum(grad * zfull, axis=-1, keepdims=True))).astype(
        jnp.bfloat16
    )


def local(images, texts, img_head, txt_head, log_scale, bias):
    img, txt = images[0], texts[0]
    c = lax.axis_index("c")
    first = c == 0
    scale = jnp.exp(log_scale)

    def swap(a):
        return lax.ppermute(a, AXES, core_swap())

    near = lax.ppermute(txt, AXES, chip_shift(1))
    other_img, other_txt = swap(img), swap(txt)
    far = lax.ppermute(jnp.where(first, other_txt[:128], txt[128:]), AXES, chip_shift(2))
    passed = swap(jnp.concatenate([near, far], axis=0))
    near_o, far_o = passed[:256], passed[256:]
    f_txt = jnp.where(
        first,
        jnp.concatenate([far, far_o, near, near_o, txt, other_txt], axis=0),
        jnp.concatenate([far_o, far, near_o, near, other_txt, txt], axis=0),
    )
    f_img = jnp.where(
        first, jnp.concatenate([img, other_img], 0), jnp.concatenate([other_img, img], 0)
    )
    zf_img, inv_img = normed(f_img, img_head)
    zf_txt, inv_txt = normed(f_txt, txt_head)
    z_img = zf_img.astype(jnp.bfloat16)
    z_txt = zf_txt.astype(jnp.bfloat16)

    col = lax.broadcasted_iota(jnp.int32, (BLOCK, 4 * BLOCK), 1)
    row = lax.broadcasted_iota(jnp.int32, (BLOCK, 4 * BLOCK), 0)
    labels = jnp.where(col == row + 3 * BLOCK, 1.0, -1.0)
    losses, g_img, g_txt = [], [], jnp.zeros((5 * BLOCK, 1152), jnp.float32)
    for d in range(2):
        q = z_img[d * BLOCK : (d + 1) * BLOCK]
        k = z_txt[d * BLOCK : (d + 4) * BLOCK]
        logits = scale * jnp.dot(q, k.T, preferred_element_type=jnp.float32) + bias
        gt = (scale * (-labels * jax.nn.sigmoid(-labels * logits)) / BLOCK).astype(jnp.bfloat16)
        losses.append(jnp.sum(jax.nn.softplus(-labels * logits), axis=1))
        g_img.append(jnp.dot(gt, k, preferred_element_type=jnp.float32))
        dk = jnp.dot(gt.T, q, preferred_element_type=jnp.float32)
        g_txt = g_txt.at[d * BLOCK : (d + 4) * BLOCK].add(dk)
    loss = jnp.where(first, losses[0], losses[1])
    du_img = backnorm(jnp.concatenate(g_img, 0), zf_img, inv_img)
    du_txt = backnorm(g_txt, zf_txt, inv_txt)

    order = jnp.asarray(row_order())[c]
    pick = (lax.broadcasted_iota(jnp.int32, (2, 576, 1152), 2) == order[:, :, None]).astype(jnp.bfloat16)
    terms = []
    for f, du, p in ((f_img, du_img, pick[0]), (f_txt, du_txt, pick[1])):
        ft = jnp.dot(p, f.T, preferred_element_type=jnp.float32).astype(jnp.bfloat16)
        terms.append(jnp.dot(ft, du, preferred_element_type=jnp.float32).reshape(8, 72, 1152))
    term = jnp.concatenate(terms, axis=1).astype(jnp.bfloat16)
    got = lax.all_to_all(term.reshape(1152, 1152), AXES, 0, 0, axis_index_groups=first_groups(), tiled=True)
    half = jnp.sum(got.reshape(8, 16, 9, 1152).astype(jnp.float32), axis=0)
    half = half.reshape(16, 81, 128).astype(jnp.bfloat16)
    half = jnp.pad(half, ((0, 0), (0, 7), (0, 0))).reshape(16 * 88, 128)
    got = lax.all_to_all(half, AXES, 0, 0, axis_index_groups=second_groups(), tiled=True)
    shares = jnp.sum(got.reshape(16, 88, 128).astype(jnp.float32), axis=0)[:81].reshape(9, 1152)
    return (loss[None, :], shares)


def solution(mesh):
    inner = Mesh(mesh.devices.reshape(NZ, NY, 2, 2, 2), AXES)
    dp = ("z", "y", "xh", "c")
    placed = (P("xl", dp, None), P("xl", dp, None), P(), P(), P(), P())
    return jax.shard_map(
        local,
        mesh=inner,
        in_specs=placed,
        out_specs=(P("xl", dp), P(AXES, None)),
        check_vma=False,
    )
```

```python
import jax
import jax.numpy as jnp
from jax import lax
from jax.experimental import pallas as pl
from jax.experimental.pallas import tpu as pltpu
from jax.sharding import Mesh, PartitionSpec as P

AXES = ("z", "y", "xh", "c", "xl")
NZ, NY, NX = 8, 4, 4
BLOCK = 256
WIDTH = 1152
MIB = 1 << 20
BF16, F32 = jnp.bfloat16, jnp.float32


def place(i):
    return i // 32, (i // 8) % 4, ((i // 4) % 2) * 2 + i % 2, (i // 2) % 2


def index(z, y, x, c):
    return (((z * NY + y) * 2 + x // 2) * 2 + c) * 2 + x % 2


def chip_shift(by):
    pairs = []
    for i in range(256):
        z, y, x, c = place(i)
        q = (((z * NY + y) * 2 + x // 2) + by) % 64
        pairs.append((i, index(q // 8, (q // 2) % 4, (q % 2) * 2 + x % 2, c)))
    return pairs


def core_swap():
    return [(i, index(*place(i)[:3], 1 - place(i)[3])) for i in range(256)]


def grouped(key, order):
    found = {}
    for i in range(256):
        found.setdefault(key(*place(i)), []).append(i)
    return [sorted(v, key=lambda i: order(*place(i))) for v in found.values()]


def first_groups():
    return grouped(
        lambda z, y, x, c: (c, y, z // 2) if c == 0 else (c, x, ((z + 1) % NZ) // 2),
        lambda z, y, x, c: (z % 2, x if c == 0 else y),
    )


def second_groups():
    return grouped(
        lambda z, y, x, c: (c, x if c == 0 else y, z % 2),
        lambda z, y, x, c: (z // 2, y if c == 0 else x),
    )


def head_rows(c):
    r = lax.broadcasted_iota(jnp.int32, (576, 1), 0)

    def digit(r, size, count):
        d = sum((r >= size * k).astype(jnp.int32) for k in range(1, count))
        return d, r - size * d

    zl, r = digit(r, 288, 2)
    a, r = digit(r, 72, 4)
    zh, r = digit(r, 36, 2)
    b, r = digit(r, 9, 4)
    x, y = jnp.where(c == 0, a, b), jnp.where(c == 0, b, a)
    device = (((2 * zh + zl) * 4 + y) * 2 + (x >> 1)) * 4 + c * 2 + (x & 1)
    return 9 * device + r


def dot(a, b, contract=((1,), (0,))):
    return lax.dot_general(a, b, (contract, ((), ())), preferred_element_type=jnp.float32)


NT = ((1,), (1,))
TN = ((0,), (0,))


def normalise(feats, head):
    u = dot(feats, head)
    inv = lax.rsqrt(jnp.sum(u * u, axis=-1, keepdims=True) + 1e-06)
    return u * inv, inv


def rest(zf):
    return (zf - zf.astype(BF16).astype(F32)).astype(BF16)


def backnorm(grad, zfull, inv):
    return (inv * (grad - zfull * jnp.sum(grad * zfull, axis=-1, keepdims=True))).astype(BF16)


def score(query, keys, scale, bias, diagonal, gt_ref, loss_ref, wanted):
    logits = scale * dot(query, keys, NT) + bias
    if diagonal is not None:
        row = lax.broadcasted_iota(jnp.int32, logits.shape, 0)
        col = lax.broadcasted_iota(jnp.int32, logits.shape, 1)
        own = col == row + diagonal
        logits = jnp.where(own, -logits, logits)
    e = jnp.exp(-jnp.abs(logits))
    sig = jnp.where(logits >= 0, 1.0, e) / (1.0 + e)
    if diagonal is not None:
        sig = jnp.where(own, -sig, sig)
    gt_ref[...] = (scale * sig / BLOCK).astype(BF16)

    @pl.when(wanted)
    def _():
        loss_ref[...] += jnp.sum(jnp.maximum(logits, 0.0) + jnp.log1p(e), axis=1, keepdims=True)


def early_kernel(
    core_ref, par_ref, img, txt, oimg, otxt, himg_hbm, htxt_hbm,
    zi, lzi, inv, dq, fti, pick, loss, z4, lz4, inv4, g4, ft34, du3,
    himg, htxt, fimg, ftxt, zt, zf3, gts, sems,
):
    c = core_ref[0]
    mine, other = pl.multiple_of(c * BLOCK, BLOCK), pl.multiple_of((1 - c) * BLOCK, BLOCK)
    copies = [
        pltpu.make_async_copy(src, dst, sems.at[k])
        for k, (src, dst) in enumerate((
            (img, fimg.at[pl.ds(mine, BLOCK)]), (oimg, fimg.at[pl.ds(other, BLOCK)]), (himg_hbm, himg),
            (txt, ftxt.at[pl.ds(mine, BLOCK)]), (otxt, ftxt.at[pl.ds(other, BLOCK)]), (htxt_hbm, htxt),
        ))
    ]
    for copy in copies:
        copy.start()
    scale, bias = par_ref[0], par_ref[1]
    pick[...] = (lax.broadcasted_iota(jnp.int32, (576, WIDTH), 1) == head_rows(c)).astype(BF16)
    loss[...] = jnp.zeros_like(loss)
    lo, hi = slice(0, BLOCK), slice(BLOCK, 2 * BLOCK)
    for copy in copies[:3]:
        copy.wait()
    fti[...] = dot(pick[...], fimg[...], NT).astype(BF16)
    for rows in (lo, hi):
        zf, i = normalise(fimg[rows], himg[...])
        lzi[rows] = rest(zf)
        zi[rows] = zf.astype(BF16)
        inv[rows] = i
    for copy in copies[3:]:
        copy.wait()
    ft34[...] = dot(pick[...], ftxt[...], NT).astype(BF16)
    zf, inv3 = normalise(ftxt[lo], htxt[...])
    zf3[...] = zf
    zt[lo] = zf.astype(BF16)
    zf, i = normalise(ftxt[hi], htxt[...])
    lz4[...] = rest(zf)
    zt[hi] = zf.astype(BF16)
    z4[...] = zt[hi]
    inv4[...] = i
    score(zi[lo], zt[lo], scale, bias, 0, gts.at[lo, lo], loss, c == 0)
    score(zi[hi], zt[...], scale, bias, BLOCK, gts.at[hi, :], loss, c == 1)
    dq[lo] = dot(gts[lo, lo], zt[lo])
    dq[hi] = dot(gts[hi, :], zt[...])
    du3[...] = backnorm(dot(gts[:, lo], zi[...], TN), zf3[...], inv3)
    g4[...] = dot(gts[hi, hi], zi[hi], TN)


def late_kernel(
    core_ref, par_ref, near, near_o, far, far_o,
    himg, htxt, zi, lzi, inv, dq, fti, pick, loss_near, z4, lz4, inv4, g4, ft34, du3,
    out, loss_out, loss_far,
    ft, f2, zt, zft, z2, zf2, gts, gt2, loss, loss2, du_i, du_t, ftt, ft2,
):
    c = core_ref[0]
    f2[pl.ds(pl.multiple_of(c * 128, 128), 128)] = far[...]
    f2[pl.ds(pl.multiple_of((1 - c) * 128, 128), 128)] = far_o[...]
    ft[pl.ds(pl.multiple_of(c * BLOCK, BLOCK), BLOCK)] = near[...]
    ft[pl.ds(pl.multiple_of((1 - c) * BLOCK, BLOCK), BLOCK)] = near_o[...]
    scale, bias = par_ref[0], par_ref[1]
    lo, hi, end = slice(0, BLOCK), slice(BLOCK, 2 * BLOCK), slice(2 * BLOCK, 3 * BLOCK)
    zf, inv2 = normalise(f2[...], himg[...])
    zf2[...] = zf
    z2[...] = zf.astype(BF16)
    inv_t = []
    for rows in (lo, hi):
        zf, i = normalise(ft[rows], htxt[...])
        zft[rows] = zf
        zt[rows] = zf.astype(BF16)
        inv_t.append(i)
    ft2[...] = dot(pick[...], f2[...], NT).astype(BF16)
    ftt[...] = dot(pick[...], ft[...], NT).astype(BF16)
    loss[...] = loss_near[...]
    loss2[...] = jnp.zeros_like(loss2)
    score(z2[...], z4[...], scale, bias, None, gt2, loss2, c == 0)
    score(zi[lo], zt[...], scale, bias, None, gts.at[lo, :], loss, c == 0)
    score(zi[hi], zt[...], scale, bias, None, gts.at[hi, :], loss, c == 1)
    loss_out[...] = jnp.transpose(jnp.broadcast_to(loss[...], (BLOCK, 128)))[:1]
    loss_far[...] = jnp.transpose(jnp.broadcast_to(loss2[...], (BLOCK, 128)))[:1]
    du_i[end] = backnorm(dot(gt2[...], z4[...]), zf2[...], inv2)
    du_t[2 * BLOCK : 3 * BLOCK] = du3[...]
    du_t[3 * BLOCK :] = backnorm(g4[...] + dot(gt2[...], z2[...], TN), z4[...].astype(F32) + lz4[...], inv4[...])
    for rows, inv_k in zip((lo, hi), inv_t):
        du_i[rows] = backnorm(dq[rows] + dot(gts[rows, :], zt[...]), zi[rows].astype(F32) + lzi[rows], inv[rows])
        du_t[rows] = backnorm(dot(gts[:, rows], zi[...], TN), zft[rows], inv_k)
    for first in range(0, WIDTH, 256):
        cols = slice(first, min(first + 256, WIDTH))
        g_i = dot(fti[...], du_i[: 2 * BLOCK, cols]) + dot(ft2[...], du_i[end, cols])
        g_t = dot(ftt[...], du_t[: 2 * BLOCK, cols]) + dot(ft34[...], du_t[2 * BLOCK :, cols])
        wide = g_i.shape[1]
        both = jnp.concatenate([g_i.reshape(8, 72, wide), g_t.reshape(8, 72, wide)], axis=1)
        out[:, cols] = both.reshape(WIDTH, wide).astype(BF16)


def half_kernel(got, out, total, parts):
    acc = got[0:144].astype(F32)
    for j in range(1, 8):
        acc += got[144 * j : 144 * (j + 1)].astype(F32)
    total[...] = acc
    parts[...] = jnp.zeros_like(parts)
    for m in range(16):
        for l in range(9):
            parts[88 * m + 9 * l : 88 * m + 9 * l + 9] = total[9 * m : 9 * m + 9, 128 * l : 128 * (l + 1)]
    out[...] = parts[...].astype(BF16)


def last_kernel(core_ref, got, loss, loss_far, out, loss_out, total):
    values = got[...].astype(F32)
    acc = values[:88]
    for j in range(1, 16):
        acc += values[88 * j : 88 * (j + 1)]
    total[...] = acc
    for l in range(9):
        out[:, 128 * l : 128 * (l + 1)] = total[9 * l : 9 * l + 9]
    loss_out[...] = loss[...] + jnp.where(core_ref[0] == 0, loss_far[...], 0.0)


def call(kernel, out_shape, scratch, flops, spaces, limit=24 * MIB):
    vmem = pl.BlockSpec(memory_space=pltpu.VMEM)
    spec = {"s": pl.BlockSpec(memory_space=pltpu.SMEM), "v": vmem, "h": pl.BlockSpec(memory_space=pltpu.HBM)}
    return pl.pallas_call(
        kernel,
        out_shape=out_shape,
        in_specs=[spec[k] for k in spaces],
        out_specs=jax.tree.map(lambda _: vmem, out_shape),
        scratch_shapes=scratch,
        compiler_params=pltpu.CompilerParams(vmem_limit_bytes=limit),
        cost_estimate=pl.CostEstimate(flops=flops, bytes_accessed=8 * MIB, transcendentals=0),
    )


def shapes(dtype, *dims):
    return [jax.ShapeDtypeStruct(d, dtype) for d in dims]


def scratches(dtype, *dims):
    return [pltpu.VMEM(d, dtype) for d in dims]


def local(images, texts, img_head, txt_head, log_scale, bias):
    img, txt = images[0], texts[0]
    c = lax.axis_index("c")
    first = c == 0
    core = jnp.reshape(c, (1,)).astype(jnp.int32)
    params = jnp.stack([jnp.exp(log_scale), bias])

    def swap(a):
        return lax.ppermute(a, AXES, core_swap())

    near = lax.ppermute(txt, AXES, chip_shift(1))
    other_img = swap(img)
    far = lax.ppermute(jnp.where(first, img[:128], other_img[128:]), AXES, chip_shift(-2))
    other_txt = swap(txt)

    one, two, three = (BLOCK, WIDTH), (2 * BLOCK, WIDTH), (3 * BLOCK, WIDTH)
    square, head, column = (WIDTH, WIDTH), (576, WIDTH), (BLOCK, 1)
    kept = call(
        early_kernel,
        shapes(BF16, two, two) + shapes(F32, (512, 1), two) + shapes(BF16, (576, 512))
        + shapes(BF16, head) + shapes(F32, column) + shapes(BF16, one, one)
        + shapes(F32, column, one) + shapes(BF16, (576, 512), one),
        scratches(BF16, square, square, two, two, two) + scratches(F32, one)
        + scratches(BF16, (512, 512)) + [pltpu.SemaphoreType.DMA((6,))],
        2 * 9 * 340_000_000, "ssvvvvhh", 40 * MIB,
    )(core, params, img, txt, other_img, other_txt, img_head, txt_head)

    near, far, *kept = lax.optimization_barrier((near, far, *kept))
    near_o, far_o = swap(near), swap(far)
    term, loss, loss_far = call(
        late_kernel,
        shapes(BF16, square) + shapes(F32, (1, BLOCK), (1, BLOCK)),
        scratches(BF16, two, one, two) + scratches(F32, two) + scratches(BF16, one) + scratches(F32, one)
        + scratches(BF16, (512, 512), (BLOCK, BLOCK)) + scratches(F32, column, column)
        + scratches(BF16, three, (4 * BLOCK, WIDTH), (576, 512), (576, BLOCK)),
        2 * 10 * 340_000_000, "ss" + "v" * 19,
    )(core, params, near, near_o, far, far_o, img_head, txt_head, *kept)

    loss_far = lax.ppermute(loss_far, AXES, chip_shift(2))
    got = lax.all_to_all(term, AXES, 0, 0, axis_index_groups=first_groups(), tiled=True)
    (half,) = call(
        half_kernel, shapes(BF16, (1408, 128)), scratches(F32, (144, WIDTH), (1408, 128)), 10_000_000, "v",
    )(got)
    got = lax.all_to_all(half, AXES, 0, 0, axis_index_groups=second_groups(), tiled=True)
    shares, loss = call(
        last_kernel, shapes(F32, (9, WIDTH), (1, BLOCK)), scratches(F32, (88, 128)), 1_000_000, "svvv",
    )(core, got, loss, loss_far)
    return (loss, shares)


def solution(mesh):
    inner = Mesh(mesh.devices.reshape(NZ, NY, 2, 2, 2), AXES)
    dp = ("z", "y", "xh", "c")
    placed = (P("xl", dp, None), P("xl", dp, None), P(), P(), P(), P())
    return jax.shard_map(
        local,
        mesh=inner,
        in_specs=placed,
        out_specs=(P("xl", dp), P(AXES, None)),
        check_vma=False,
    )
```

```python
import jax
import jax.numpy as jnp
from jax import lax
from jax.experimental import pallas as pl
from jax.experimental.pallas import tpu as pltpu
from jax.sharding import Mesh, PartitionSpec as P

AXES = ("z", "y", "xh", "c", "xl")
NZ, NY, NX = 8, 4, 4
BLOCK = 256
WIDTH = 1152
MIB = 1 << 20
BF16, F32 = jnp.bfloat16, jnp.float32


def place(i):
    return i // 32, (i // 8) % 4, ((i // 4) % 2) * 2 + i % 2, (i // 2) % 2


def index(z, y, x, c):
    return (((z * NY + y) * 2 + x // 2) * 2 + c) * 2 + x % 2


def chip_shift(by):
    pairs = []
    for i in range(256):
        z, y, x, c = place(i)
        q = (((z * NY + y) * 2 + x // 2) + by) % 64
        pairs.append((i, index(q // 8, (q // 2) % 4, (q % 2) * 2 + x % 2, c)))
    return pairs


def core_swap():
    return [(i, index(*place(i)[:3], 1 - place(i)[3])) for i in range(256)]


def grouped(key, order):
    found = {}
    for i in range(256):
        found.setdefault(key(*place(i)), []).append(i)
    return [sorted(v, key=lambda i: order(*place(i))) for v in found.values()]


def first_groups():
    return grouped(
        lambda z, y, x, c: (c, y, z // 2) if c == 0 else (c, x, ((z + 1) % NZ) // 2),
        lambda z, y, x, c: (z % 2, x if c == 0 else y),
    )


def second_groups():
    return grouped(
        lambda z, y, x, c: (c, x if c == 0 else y, z % 2),
        lambda z, y, x, c: (z // 2, y if c == 0 else x),
    )


def head_rows(c):
    r = lax.broadcasted_iota(jnp.int32, (576, 1), 0)

    def digit(r, size, count):
        d = sum((r >= size * k).astype(jnp.int32) for k in range(1, count))
        return d, r - size * d

    zl, r = digit(r, 288, 2)
    a, r = digit(r, 72, 4)
    zh, r = digit(r, 36, 2)
    b, r = digit(r, 9, 4)
    x, y = jnp.where(c == 0, a, b), jnp.where(c == 0, b, a)
    device = (((2 * zh + zl) * 4 + y) * 2 + (x >> 1)) * 4 + c * 2 + (x & 1)
    return 9 * device + r


def dot(a, b, contract=((1,), (0,))):
    return lax.dot_general(a, b, (contract, ((), ())), preferred_element_type=jnp.float32)


NT = ((1,), (1,))
TN = ((0,), (0,))


def normalise(feats, head):
    u = dot(feats, head)
    inv = lax.rsqrt(jnp.sum(u * u, axis=-1, keepdims=True) + 1e-06)
    return u * inv, inv


def rest(zf):
    return (zf - zf.astype(BF16).astype(F32)).astype(BF16)


def backnorm(grad, zfull, inv):
    return (inv * (grad - zfull * jnp.sum(grad * zfull, axis=-1, keepdims=True))).astype(BF16)


def score(query, keys, scale, bias, diagonal, gt_ref, loss_ref, wanted):
    logits = scale * dot(query, keys, NT) + bias
    if diagonal is not None:
        row = lax.broadcasted_iota(jnp.int32, logits.shape, 0)
        col = lax.broadcasted_iota(jnp.int32, logits.shape, 1)
        own = col == row + diagonal
        logits = jnp.where(own, -logits, logits)
    e = jnp.exp(-jnp.abs(logits))
    sig = jnp.where(logits >= 0, 1.0, e) / (1.0 + e)
    if diagonal is not None:
        sig = jnp.where(own, -sig, sig)
    gt_ref[...] = (scale * sig / BLOCK).astype(BF16)

    @pl.when(wanted)
    def _():
        loss_ref[...] += jnp.sum(jnp.maximum(logits, 0.0) + jnp.log1p(e), axis=1, keepdims=True)


LO, HI, END = (slice(k * BLOCK, (k + 1) * BLOCK) for k in range(3))


def early_kernel(
    core_ref, par_ref, img, txt, oimg, otxt, himg_hbm, htxt_hbm,
    zi, lzi, inv, fti, pick, zt, lzt, invt, ft34,
    himg, htxt, fimg, ftxt, sems,
):
    c = core_ref[0]
    mine, other = pl.multiple_of(c * BLOCK, BLOCK), pl.multiple_of((1 - c) * BLOCK, BLOCK)
    copies = [
        pltpu.make_async_copy(src, dst, sems.at[k])
        for k, (src, dst) in enumerate((
            (img, fimg.at[pl.ds(mine, BLOCK)]), (oimg, fimg.at[pl.ds(other, BLOCK)]), (himg_hbm, himg),
            (txt, ftxt.at[pl.ds(mine, BLOCK)]), (otxt, ftxt.at[pl.ds(other, BLOCK)]), (htxt_hbm, htxt),
        ))
    ]
    for copy in copies:
        copy.start()
    pick[...] = (lax.broadcasted_iota(jnp.int32, (576, WIDTH), 1) == head_rows(c)).astype(BF16)
    for f, ft, head, z, lz, i, waits in (
        (fimg, fti, himg, zi, lzi, inv, copies[:3]), (ftxt, ft34, htxt, zt, lzt, invt, copies[3:]),
    ):
        for copy in waits:
            copy.wait()
        ft[...] = dot(pick[...], f[...], NT).astype(BF16)
        for rows in (LO, HI):
            zf, i[rows] = normalise(f[rows], head[...])
            lz[rows] = rest(zf)
            z[rows] = zf.astype(BF16)


def own_kernel(core_ref, par_ref, zi, zt, lzt, invt, loss, dq, g4, du3, gts):
    c = core_ref[0]
    scale, bias = par_ref[0], par_ref[1]
    loss[...] = jnp.zeros_like(loss)
    score(zi[LO], zt[LO], scale, bias, 0, gts.at[LO, LO], loss, c == 0)
    score(zi[HI], zt[...], scale, bias, BLOCK, gts.at[HI, :], loss, c == 1)
    dq[LO] = dot(gts[LO, LO], zt[LO])
    dq[HI] = dot(gts[HI, :], zt[...])
    du3[...] = backnorm(dot(gts[:, LO], zi[...], TN), zt[LO].astype(F32) + lzt[LO], invt[LO])
    g4[...] = dot(gts[HI, HI], zi[HI], TN)


def late_kernel(
    core_ref, par_ref, near, near_o, far, far_o,
    himg, htxt, zi, lzi, inv, fti, pick, zown, lzown, invown, ft34, loss_near, dq, g4, du3,
    out, loss_out, loss_far,
    ft, f2, zt, zft, z2, zf2, gts, gt2, loss, loss2, du_i, du_t, ftt, ft2,
):
    c = core_ref[0]
    f2[pl.ds(pl.multiple_of(c * 128, 128), 128)] = far[...]
    f2[pl.ds(pl.multiple_of((1 - c) * 128, 128), 128)] = far_o[...]
    ft[pl.ds(pl.multiple_of(c * BLOCK, BLOCK), BLOCK)] = near[...]
    ft[pl.ds(pl.multiple_of((1 - c) * BLOCK, BLOCK), BLOCK)] = near_o[...]
    scale, bias = par_ref[0], par_ref[1]
    lo, hi, end = slice(0, BLOCK), slice(BLOCK, 2 * BLOCK), slice(2 * BLOCK, 3 * BLOCK)
    zf, inv2 = normalise(f2[...], himg[...])
    zf2[...] = zf
    z2[...] = zf.astype(BF16)
    inv_t = []
    for rows in (lo, hi):
        zf, i = normalise(ft[rows], htxt[...])
        zft[rows] = zf
        zt[rows] = zf.astype(BF16)
        inv_t.append(i)
    ft2[...] = dot(pick[...], f2[...], NT).astype(BF16)
    ftt[...] = dot(pick[...], ft[...], NT).astype(BF16)
    loss[...] = loss_near[...]
    loss2[...] = jnp.zeros_like(loss2)
    score(z2[...], zown[HI], scale, bias, None, gt2, loss2, c == 0)
    score(zi[lo], zt[...], scale, bias, None, gts.at[lo, :], loss, c == 0)
    score(zi[hi], zt[...], scale, bias, None, gts.at[hi, :], loss, c == 1)
    loss_out[...] = jnp.transpose(jnp.broadcast_to(loss[...], (BLOCK, 128)))[:1]
    loss_far[...] = jnp.transpose(jnp.broadcast_to(loss2[...], (BLOCK, 128)))[:1]
    du_i[end] = backnorm(dot(gt2[...], zown[HI]), zf2[...], inv2)
    du_t[2 * BLOCK : 3 * BLOCK] = du3[...]
    du_t[3 * BLOCK :] = backnorm(g4[...] + dot(gt2[...], z2[...], TN), zown[HI].astype(F32) + lzown[HI], invown[HI])
    for rows, inv_k in zip((lo, hi), inv_t):
        du_i[rows] = backnorm(dq[rows] + dot(gts[rows, :], zt[...]), zi[rows].astype(F32) + lzi[rows], inv[rows])
        du_t[rows] = backnorm(dot(gts[:, rows], zi[...], TN), zft[rows], inv_k)
    for first in range(0, WIDTH, 256):
        cols = slice(first, min(first + 256, WIDTH))
        g_i = dot(fti[...], du_i[: 2 * BLOCK, cols]) + dot(ft2[...], du_i[end, cols])
        g_t = dot(ftt[...], du_t[: 2 * BLOCK, cols]) + dot(ft34[...], du_t[2 * BLOCK :, cols])
        wide = g_i.shape[1]
        both = jnp.concatenate([g_i.reshape(8, 72, wide), g_t.reshape(8, 72, wide)], axis=1)
        out[:, cols] = both.reshape(WIDTH, wide).astype(BF16)


def half_kernel(got, out, total, parts):
    acc = got[0:144].astype(F32)
    for j in range(1, 8):
        acc += got[144 * j : 144 * (j + 1)].astype(F32)
    total[...] = acc
    parts[...] = jnp.zeros_like(parts)
    for m in range(16):
        for l in range(9):
            parts[88 * m + 9 * l : 88 * m + 9 * l + 9] = total[9 * m : 9 * m + 9, 128 * l : 128 * (l + 1)]
    out[...] = parts[...].astype(BF16)


def last_kernel(core_ref, got, loss, loss_far, out, loss_out, total):
    values = got[...].astype(F32)
    acc = values[:88]
    for j in range(1, 16):
        acc += values[88 * j : 88 * (j + 1)]
    total[...] = acc
    for l in range(9):
        out[:, 128 * l : 128 * (l + 1)] = total[9 * l : 9 * l + 9]
    loss_out[...] = loss[...] + jnp.where(core_ref[0] == 0, loss_far[...], 0.0)


def call(kernel, out_shape, scratch, flops, spaces, limit=24 * MIB):
    vmem = pl.BlockSpec(memory_space=pltpu.VMEM)
    spec = {"s": pl.BlockSpec(memory_space=pltpu.SMEM), "v": vmem, "h": pl.BlockSpec(memory_space=pltpu.HBM)}
    return pl.pallas_call(
        kernel,
        out_shape=out_shape,
        in_specs=[spec[k] for k in spaces],
        out_specs=jax.tree.map(lambda _: vmem, out_shape),
        scratch_shapes=scratch,
        compiler_params=pltpu.CompilerParams(vmem_limit_bytes=limit),
        cost_estimate=pl.CostEstimate(flops=flops, bytes_accessed=8 * MIB, transcendentals=0),
    )


def shapes(dtype, *dims):
    return [jax.ShapeDtypeStruct(d, dtype) for d in dims]


def scratches(dtype, *dims):
    return [pltpu.VMEM(d, dtype) for d in dims]


def local(images, texts, img_head, txt_head, log_scale, bias):
    img, txt = images[0], texts[0]
    c = lax.axis_index("c")
    first = c == 0
    core = jnp.reshape(c, (1,)).astype(jnp.int32)
    params = jnp.stack([jnp.exp(log_scale), bias])

    def swap(a):
        return lax.ppermute(a, AXES, core_swap())

    near = lax.ppermute(txt, AXES, chip_shift(1))
    other_img = swap(img)
    far = lax.ppermute(jnp.where(first, img[:128], other_img[128:]), AXES, chip_shift(-2))
    other_txt = swap(txt)

    one, two, three = (BLOCK, WIDTH), (2 * BLOCK, WIDTH), (3 * BLOCK, WIDTH)
    square, head, column = (WIDTH, WIDTH), (576, WIDTH), (BLOCK, 1)
    kept = call(
        early_kernel,
        shapes(BF16, two, two) + shapes(F32, (512, 1)) + shapes(BF16, (576, 512), head, two, two)
        + shapes(F32, (512, 1)) + shapes(BF16, (576, 512)),
        scratches(BF16, square, square, two, two) + [pltpu.SemaphoreType.DMA((6,))],
        2 * 6 * 340_000_000, "ssvvvvhh", 44 * MIB,
    )(core, params, img, txt, other_img, other_txt, img_head, txt_head)

    near, far, *kept = lax.optimization_barrier((near, far, *kept))
    near_o, far_o = swap(near), swap(far)
    zi, zt, lzt, invt = kept[0], kept[5], kept[6], kept[7]
    own = call(
        own_kernel,
        shapes(F32, column, two, one) + shapes(BF16, one), scratches(BF16, (512, 512)),
        2 * 2 * 340_000_000, "ssvvvv", 8 * MIB,
    )(core, params, zi, zt, lzt, invt)
    term, loss, loss_far = call(
        late_kernel,
        shapes(BF16, square) + shapes(F32, (1, BLOCK), (1, BLOCK)),
        scratches(BF16, two, one, two) + scratches(F32, two) + scratches(BF16, one) + scratches(F32, one)
        + scratches(BF16, (512, 512), (BLOCK, BLOCK)) + scratches(F32, column, column)
        + scratches(BF16, three, (4 * BLOCK, WIDTH), (576, 512), (576, BLOCK)),
        2 * 10 * 340_000_000, "ss" + "v" * 19,
    )(core, params, near, near_o, far, far_o, img_head, txt_head, *kept, *own)

    loss_far = lax.ppermute(loss_far, AXES, chip_shift(2))
    got = lax.all_to_all(term, AXES, 0, 0, axis_index_groups=first_groups(), tiled=True)
    (half,) = call(
        half_kernel, shapes(BF16, (1408, 128)), scratches(F32, (144, WIDTH), (1408, 128)), 10_000_000, "v",
    )(got)
    got = lax.all_to_all(half, AXES, 0, 0, axis_index_groups=second_groups(), tiled=True)
    shares, loss = call(
        last_kernel, shapes(F32, (9, WIDTH), (1, BLOCK)), scratches(F32, (88, 128)), 1_000_000, "svvv",
    )(core, got, loss, loss_far)
    return (loss, shares)


def solution(mesh):
    inner = Mesh(mesh.devices.reshape(NZ, NY, 2, 2, 2), AXES)
    dp = ("z", "y", "xh", "c")
    placed = (P("xl", dp, None), P("xl", dp, None), P(), P(), P(), P())
    return jax.shard_map(
        local,
        mesh=inner,
        in_specs=placed,
        out_specs=(P("xl", dp), P(AXES, None)),
        check_vma=False,
    )
```

```python
import jax
import jax.numpy as jnp
from jax import lax
from jax.experimental import pallas as pl
from jax.experimental.pallas import tpu as pltpu
from jax.sharding import Mesh, PartitionSpec as P

AXES = ("z", "y", "xh", "c", "xl")
NZ, NY, NX = 8, 4, 4
BLOCK = 256
WIDTH = 1152
MIB = 1 << 20
BF16, F32 = jnp.bfloat16, jnp.float32


def place(i):
    return i // 32, (i // 8) % 4, ((i // 4) % 2) * 2 + i % 2, (i // 2) % 2


def index(z, y, x, c):
    return (((z * NY + y) * 2 + x // 2) * 2 + c) * 2 + x % 2


def chip_shift(by):
    pairs = []
    for i in range(256):
        z, y, x, c = place(i)
        q = (((z * NY + y) * 2 + x // 2) + by) % 64
        pairs.append((i, index(q // 8, (q // 2) % 4, (q % 2) * 2 + x % 2, c)))
    return pairs


def core_swap():
    return [(i, index(*place(i)[:3], 1 - place(i)[3])) for i in range(256)]


def grouped(key, order):
    found = {}
    for i in range(256):
        found.setdefault(key(*place(i)), []).append(i)
    return [sorted(v, key=lambda i: order(*place(i))) for v in found.values()]


def first_groups():
    return grouped(
        lambda z, y, x, c: (c, y, z // 2) if c == 0 else (c, x, ((z + 1) % NZ) // 2),
        lambda z, y, x, c: (z % 2, x if c == 0 else y),
    )


def second_groups():
    return grouped(
        lambda z, y, x, c: (c, x if c == 0 else y, z % 2),
        lambda z, y, x, c: (z // 2, y if c == 0 else x),
    )


def head_rows(c):
    r = lax.broadcasted_iota(jnp.int32, (576, 1), 0)

    def digit(r, size, count):
        d = sum((r >= size * k).astype(jnp.int32) for k in range(1, count))
        return d, r - size * d

    zl, r = digit(r, 288, 2)
    a, r = digit(r, 72, 4)
    zh, r = digit(r, 36, 2)
    b, r = digit(r, 9, 4)
    x, y = jnp.where(c == 0, a, b), jnp.where(c == 0, b, a)
    device = (((2 * zh + zl) * 4 + y) * 2 + (x >> 1)) * 4 + c * 2 + (x & 1)
    return 9 * device + r


def dot(a, b, contract=((1,), (0,))):
    return lax.dot_general(a, b, (contract, ((), ())), preferred_element_type=jnp.float32)


NT = ((1,), (1,))
TN = ((0,), (0,))


def normalise(feats, head):
    u = dot(feats, head)
    inv = lax.rsqrt(jnp.sum(u * u, axis=-1, keepdims=True) + 1e-06)
    return u * inv, inv


def rest(zf):
    return (zf - zf.astype(BF16).astype(F32)).astype(BF16)


def backnorm(grad, zfull, inv):
    return (inv * (grad - zfull * jnp.sum(grad * zfull, axis=-1, keepdims=True))).astype(BF16)


def score(query, keys, scale, bias, diagonal, gt_ref, loss_ref, wanted):
    logits = scale * dot(query, keys, NT) + bias
    if diagonal is not None:
        row = lax.broadcasted_iota(jnp.int32, logits.shape, 0)
        col = lax.broadcasted_iota(jnp.int32, logits.shape, 1)
        own = col == row + diagonal
        logits = jnp.where(own, -logits, logits)
    e = jnp.exp(-jnp.abs(logits))
    sig = jnp.where(logits >= 0, 1.0, e) / (1.0 + e)
    if diagonal is not None:
        sig = jnp.where(own, -sig, sig)
    gt_ref[...] = (scale * sig / BLOCK).astype(BF16)

    @pl.when(wanted)
    def _():
        loss_ref[...] += jnp.sum(jnp.maximum(logits, 0.0) + jnp.log1p(e), axis=1, keepdims=True)


LO, HI, END = (slice(k * BLOCK, (k + 1) * BLOCK) for k in range(3))


def early_kernel(
    core_ref, par_ref, img, txt, oimg, otxt, himg_hbm, htxt_hbm,
    zi, lzi, inv, fti, pick, zt, lzt, invt, ft34,
    himg, htxt, fimg, ftxt, sems,
):
    c = core_ref[0]
    mine, other = pl.multiple_of(c * BLOCK, BLOCK), pl.multiple_of((1 - c) * BLOCK, BLOCK)
    copies = [
        pltpu.make_async_copy(src, dst, sems.at[k])
        for k, (src, dst) in enumerate((
            (img, fimg.at[pl.ds(mine, BLOCK)]), (oimg, fimg.at[pl.ds(other, BLOCK)]), (himg_hbm, himg),
            (txt, ftxt.at[pl.ds(mine, BLOCK)]), (otxt, ftxt.at[pl.ds(other, BLOCK)]), (htxt_hbm, htxt),
        ))
    ]
    for copy in copies:
        copy.start()
    pick[...] = (lax.broadcasted_iota(jnp.int32, (576, WIDTH), 1) == head_rows(c)).astype(BF16)
    for f, ft, head, z, lz, i, waits in (
        (fimg, fti, himg, zi, lzi, inv, copies[:3]), (ftxt, ft34, htxt, zt, lzt, invt, copies[3:]),
    ):
        for copy in waits:
            copy.wait()
        ft[...] = dot(pick[...], f[...], NT).astype(BF16)
        for rows in (LO, HI):
            zf, i[rows] = normalise(f[rows], head[...])
            lz[rows] = rest(zf)
            z[rows] = zf.astype(BF16)


def own_kernel(core_ref, par_ref, zi, zt, lzt, invt, loss, dq, g4, du3, gts):
    c = core_ref[0]
    scale, bias = par_ref[0], par_ref[1]
    loss[...] = jnp.zeros_like(loss)
    score(zi[LO], zt[LO], scale, bias, 0, gts.at[LO, LO], loss, c == 0)
    score(zi[HI], zt[...], scale, bias, BLOCK, gts.at[HI, :], loss, c == 1)
    dq[LO] = dot(gts[LO, LO], zt[LO])
    dq[HI] = dot(gts[HI, :], zt[...])
    du3[...] = backnorm(dot(gts[:, LO], zi[...], TN), zt[LO].astype(F32) + lzt[LO], invt[LO])
    g4[...] = dot(gts[HI, HI], zi[HI], TN)


def late_kernel(
    core_ref, par_ref, near, near_o, far, far_o,
    himg, htxt, zi, lzi, inv, fti, pick, zown, lzown, invown, ft34, loss_near, dq, g4, du3,
    out, loss_out, loss_far,
    ft, f2, zt, zft, z2, zf2, gts, gt2, loss, loss2, du_i, du_t, ftt, ft2,
):
    c = core_ref[0]
    f2[pl.ds(pl.multiple_of(c * 128, 128), 128)] = far[...]
    f2[pl.ds(pl.multiple_of((1 - c) * 128, 128), 128)] = far_o[...]
    ft[pl.ds(pl.multiple_of(c * BLOCK, BLOCK), BLOCK)] = near[...]
    ft[pl.ds(pl.multiple_of((1 - c) * BLOCK, BLOCK), BLOCK)] = near_o[...]
    scale, bias = par_ref[0], par_ref[1]
    lo, hi, end = slice(0, BLOCK), slice(BLOCK, 2 * BLOCK), slice(2 * BLOCK, 3 * BLOCK)
    zf, inv2 = normalise(f2[...], himg[...])
    zf2[...] = zf
    z2[...] = zf.astype(BF16)
    zf, inv_t = normalise(ft[...], htxt[...])
    zft[...] = zf
    zt[...] = zf.astype(BF16)
    ft2[...] = dot(pick[...], f2[...], NT).astype(BF16)
    ftt[...] = dot(pick[...], ft[...], NT).astype(BF16)
    loss[...] = loss_near[...]
    loss2[...] = jnp.zeros_like(loss2)
    score(z2[...], zown[HI], scale, bias, None, gt2, loss2, c == 0)
    score(zi[lo], zt[...], scale, bias, None, gts.at[lo, :], loss, c == 0)
    score(zi[hi], zt[...], scale, bias, None, gts.at[hi, :], loss, c == 1)
    loss_out[...] = jnp.transpose(jnp.broadcast_to(loss[...], (BLOCK, 128)))[:1]
    loss_far[...] = jnp.transpose(jnp.broadcast_to(loss2[...], (BLOCK, 128)))[:1]
    du_i[end] = backnorm(dot(gt2[...], zown[HI]), zf2[...], inv2)
    du_t[2 * BLOCK : 3 * BLOCK] = du3[...]
    du_t[3 * BLOCK :] = backnorm(g4[...] + dot(gt2[...], z2[...], TN), zown[HI].astype(F32) + lzown[HI], invown[HI])
    pair = slice(0, 2 * BLOCK)
    du_i[pair] = backnorm(dq[...] + dot(gts[...], zt[...]), zi[...].astype(F32) + lzi[...], inv[...])
    du_t[pair] = backnorm(dot(gts[...], zi[...], TN), zft[...], inv_t)
    for first in range(0, WIDTH, 256):
        cols = slice(first, min(first + 256, WIDTH))
        g_i = dot(fti[...], du_i[: 2 * BLOCK, cols]) + dot(ft2[...], du_i[end, cols])
        g_t = dot(ftt[...], du_t[: 2 * BLOCK, cols]) + dot(ft34[...], du_t[2 * BLOCK :, cols])
        wide = g_i.shape[1]
        both = jnp.concatenate([g_i.reshape(8, 72, wide), g_t.reshape(8, 72, wide)], axis=1)
        out[:, cols] = both.reshape(WIDTH, wide).astype(BF16)


def half_kernel(got, out, total, parts):
    acc = got[0:144].astype(F32)
    for j in range(1, 8):
        acc += got[144 * j : 144 * (j + 1)].astype(F32)
    total[...] = acc
    parts[...] = jnp.zeros_like(parts)
    for m in range(16):
        for l in range(9):
            parts[88 * m + 9 * l : 88 * m + 9 * l + 9] = total[9 * m : 9 * m + 9, 128 * l : 128 * (l + 1)]
    out[...] = parts[...].astype(BF16)


def last_kernel(core_ref, got, loss, loss_far, out, loss_out, total):
    values = got[...].astype(F32)
    acc = values[:88]
    for j in range(1, 16):
        acc += values[88 * j : 88 * (j + 1)]
    total[...] = acc
    for l in range(9):
        out[:, 128 * l : 128 * (l + 1)] = total[9 * l : 9 * l + 9]
    loss_out[...] = loss[...] + jnp.where(core_ref[0] == 0, loss_far[...], 0.0)


def call(kernel, out_shape, scratch, flops, spaces, limit=24 * MIB):
    vmem = pl.BlockSpec(memory_space=pltpu.VMEM)
    spec = {"s": pl.BlockSpec(memory_space=pltpu.SMEM), "v": vmem, "h": pl.BlockSpec(memory_space=pltpu.HBM)}
    return pl.pallas_call(
        kernel,
        out_shape=out_shape,
        in_specs=[spec[k] for k in spaces],
        out_specs=jax.tree.map(lambda _: vmem, out_shape),
        scratch_shapes=scratch,
        compiler_params=pltpu.CompilerParams(vmem_limit_bytes=limit),
        cost_estimate=pl.CostEstimate(flops=flops, bytes_accessed=8 * MIB, transcendentals=0),
    )


def shapes(dtype, *dims):
    return [jax.ShapeDtypeStruct(d, dtype) for d in dims]


def scratches(dtype, *dims):
    return [pltpu.VMEM(d, dtype) for d in dims]


def local(images, texts, img_head, txt_head, log_scale, bias):
    img, txt = images[0], texts[0]
    c = lax.axis_index("c")
    first = c == 0
    core = jnp.reshape(c, (1,)).astype(jnp.int32)
    params = jnp.stack([jnp.exp(log_scale), bias])

    def swap(a):
        return lax.ppermute(a, AXES, core_swap())

    near = lax.ppermute(txt, AXES, chip_shift(1))
    other_img = swap(img)
    far = lax.ppermute(jnp.where(first, img[:128], other_img[128:]), AXES, chip_shift(-2))
    other_txt = swap(txt)

    one, two, three = (BLOCK, WIDTH), (2 * BLOCK, WIDTH), (3 * BLOCK, WIDTH)
    square, head, column = (WIDTH, WIDTH), (576, WIDTH), (BLOCK, 1)
    kept = call(
        early_kernel,
        shapes(BF16, two, two) + shapes(F32, (512, 1)) + shapes(BF16, (576, 512), head, two, two)
        + shapes(F32, (512, 1)) + shapes(BF16, (576, 512)),
        scratches(BF16, square, square, two, two) + [pltpu.SemaphoreType.DMA((6,))],
        2 * 6 * 340_000_000, "ssvvvvhh", 44 * MIB,
    )(core, params, img, txt, other_img, other_txt, img_head, txt_head)

    near, far, *kept = lax.optimization_barrier((near, far, *kept))
    near_o, far_o = swap(near), swap(far)
    zi, zt, lzt, invt = kept[0], kept[5], kept[6], kept[7]
    own = call(
        own_kernel,
        shapes(F32, column, two, one) + shapes(BF16, one), scratches(BF16, (512, 512)),
        2 * 2 * 340_000_000, "ssvvvv", 8 * MIB,
    )(core, params, zi, zt, lzt, invt)
    term, loss, loss_far = call(
        late_kernel,
        shapes(BF16, square) + shapes(F32, (1, BLOCK), (1, BLOCK)),
        scratches(BF16, two, one, two) + scratches(F32, two) + scratches(BF16, one) + scratches(F32, one)
        + scratches(BF16, (512, 512), (BLOCK, BLOCK)) + scratches(F32, column, column)
        + scratches(BF16, three, (4 * BLOCK, WIDTH), (576, 512), (576, BLOCK)),
        2 * 10 * 340_000_000, "ss" + "v" * 19,
    )(core, params, near, near_o, far, far_o, img_head, txt_head, *kept, *own)

    loss_far = lax.ppermute(loss_far, AXES, chip_shift(2))
    got = lax.all_to_all(term, AXES, 0, 0, axis_index_groups=first_groups(), tiled=True)
    (half,) = call(
        half_kernel, shapes(BF16, (1408, 128)), scratches(F32, (144, WIDTH), (1408, 128)), 10_000_000, "v",
    )(got)
    got = lax.all_to_all(half, AXES, 0, 0, axis_index_groups=second_groups(), tiled=True)
    shares, loss = call(
        last_kernel, shapes(F32, (9, WIDTH), (1, BLOCK)), scratches(F32, (88, 128)), 1_000_000, "svvv",
    )(core, got, loss, loss_far)
    return (loss, shares)


def solution(mesh):
    inner = Mesh(mesh.devices.reshape(NZ, NY, 2, 2, 2), AXES)
    dp = ("z", "y", "xh", "c")
    placed = (P("xl", dp, None), P("xl", dp, None), P(), P(), P(), P())
    return jax.shard_map(
        local,
        mesh=inner,
        in_specs=placed,
        out_specs=(P("xl", dp), P(AXES, None)),
        check_vma=False,
    )
```

```python
import jax
import jax.numpy as jnp
from jax import lax
from jax.experimental import pallas as pl
from jax.experimental.pallas import tpu as pltpu
from jax.sharding import Mesh, PartitionSpec as P

AXES = ("z", "y", "xh", "c", "xl")
NZ, NY, NX = 8, 4, 4
BLOCK = 256
WIDTH = 1152
MIB = 1 << 20
BF16, F32 = jnp.bfloat16, jnp.float32


def place(i):
    return i // 32, (i // 8) % 4, ((i // 4) % 2) * 2 + i % 2, (i // 2) % 2


def index(z, y, x, c):
    return (((z * NY + y) * 2 + x // 2) * 2 + c) * 2 + x % 2


def chip_shift(by):
    pairs = []
    for i in range(256):
        z, y, x, c = place(i)
        q = (((z * NY + y) * 2 + x // 2) + by) % 64
        pairs.append((i, index(q // 8, (q // 2) % 4, (q % 2) * 2 + x % 2, c)))
    return pairs


def core_swap():
    return [(i, index(*place(i)[:3], 1 - place(i)[3])) for i in range(256)]


def grouped(key, order):
    found = {}
    for i in range(256):
        found.setdefault(key(*place(i)), []).append(i)
    return [sorted(v, key=lambda i: order(*place(i))) for v in found.values()]


def first_groups():
    return grouped(
        lambda z, y, x, c: (c, y, z // 2) if c == 0 else (c, x, ((z + 1) % NZ) // 2),
        lambda z, y, x, c: (z % 2, x if c == 0 else y),
    )


def second_groups():
    return grouped(
        lambda z, y, x, c: (c, x if c == 0 else y, z % 2),
        lambda z, y, x, c: (z // 2, y if c == 0 else x),
    )


def head_rows(c):
    r = lax.broadcasted_iota(jnp.int32, (576, 1), 0)

    def digit(r, size, count):
        d = sum((r >= size * k).astype(jnp.int32) for k in range(1, count))
        return d, r - size * d

    zl, r = digit(r, 288, 2)
    a, r = digit(r, 72, 4)
    zh, r = digit(r, 36, 2)
    b, r = digit(r, 9, 4)
    x, y = jnp.where(c == 0, a, b), jnp.where(c == 0, b, a)
    device = (((2 * zh + zl) * 4 + y) * 2 + (x >> 1)) * 4 + c * 2 + (x & 1)
    return 9 * device + r


def dot(a, b, contract=((1,), (0,))):
    return lax.dot_general(a, b, (contract, ((), ())), preferred_element_type=jnp.float32)


NT = ((1,), (1,))
TN = ((0,), (0,))


def normalise(feats, head):
    u = dot(feats, head)
    inv = lax.rsqrt(jnp.sum(u * u, axis=-1, keepdims=True) + 1e-06)
    return u * inv, inv


def rest(zf):
    return (zf - zf.astype(BF16).astype(F32)).astype(BF16)


def backnorm(grad, zfull, inv):
    return (inv * (grad - zfull * jnp.sum(grad * zfull, axis=-1, keepdims=True))).astype(BF16)


def score(query, keys, scale, bias, diagonal, gt_ref, kept):
    logits = scale * dot(query, keys, NT) + bias
    if diagonal is not None:
        row = lax.broadcasted_iota(jnp.int32, logits.shape, 0)
        col = lax.broadcasted_iota(jnp.int32, logits.shape, 1)
        own = col == row + diagonal
        logits = jnp.where(own, -logits, logits)
    kept[...] = logits
    e = jnp.exp(-jnp.abs(logits))
    sig = jnp.where(logits >= 0, 1.0, e) / (1.0 + e)
    if diagonal is not None:
        sig = jnp.where(own, -sig, sig)
    gt_ref[...] = (scale * sig / BLOCK).astype(BF16)


def softplus_rows(x):
    return jnp.sum(jnp.maximum(x, 0.0) + jnp.log1p(jnp.exp(-jnp.abs(x))), axis=1, keepdims=True)


LO, HI, END = (slice(k * BLOCK, (k + 1) * BLOCK) for k in range(3))


def early_kernel(
    core_ref, par_ref, img, txt, oimg, otxt, himg_hbm, htxt_hbm,
    zi, lzi, inv, fti, pick, zt, lzt, invt, ft34,
    himg, htxt, fimg, ftxt, sems,
):
    c = core_ref[0]
    mine, other = pl.multiple_of(c * BLOCK, BLOCK), pl.multiple_of((1 - c) * BLOCK, BLOCK)
    copies = [
        pltpu.make_async_copy(src, dst, sems.at[k])
        for k, (src, dst) in enumerate((
            (img, fimg.at[pl.ds(mine, BLOCK)]), (oimg, fimg.at[pl.ds(other, BLOCK)]), (himg_hbm, himg),
            (txt, ftxt.at[pl.ds(mine, BLOCK)]), (otxt, ftxt.at[pl.ds(other, BLOCK)]), (htxt_hbm, htxt),
        ))
    ]
    for copy in copies:
        copy.start()
    pick[...] = (lax.broadcasted_iota(jnp.int32, (576, WIDTH), 1) == head_rows(c)).astype(BF16)
    for f, ft, head, z, lz, i, waits in (
        (fimg, fti, himg, zi, lzi, inv, copies[:3]), (ftxt, ft34, htxt, zt, lzt, invt, copies[3:]),
    ):
        for copy in waits:
            copy.wait()
        ft[...] = dot(pick[...], f[...], NT).astype(BF16)
        zf, i[...] = normalise(f[...], head[...])
        lz[...] = rest(zf)
        z[...] = zf.astype(BF16)


def own_kernel(core_ref, par_ref, zi, zt, lzt, invt, loss, dq, g4, du3, gts, kept):
    c = core_ref[0]
    scale, bias = par_ref[0], par_ref[1]
    kept[LO, HI] = jnp.full((BLOCK, BLOCK), -1e30, F32)
    score(zi[LO], zt[LO], scale, bias, 0, gts.at[LO, LO], kept.at[LO, LO])
    score(zi[HI], zt[...], scale, bias, BLOCK, gts.at[HI, :], kept.at[HI, :])
    loss[...] = softplus_rows(kept[pl.ds(pl.multiple_of(c * BLOCK, BLOCK), BLOCK)])
    dq[LO] = dot(gts[LO, LO], zt[LO])
    dq[HI] = dot(gts[HI, :], zt[...])
    du3[...] = backnorm(dot(gts[:, LO], zi[...], TN), zt[LO].astype(F32) + lzt[LO], invt[LO])
    g4[...] = dot(gts[HI, HI], zi[HI], TN)


def late_kernel(
    core_ref, par_ref, near, near_o, far, far_o,
    himg, htxt, zi, lzi, inv, fti, pick, zown, lzown, invown, ft34, loss_near, dq, g4, du3,
    out, loss_out, loss_far,
    ft, f2, zt, zft, z2, zf2, gts, gt2, kept, kept2, du_i, du_t, ftt, ft2,
):
    c = core_ref[0]
    f2[pl.ds(pl.multiple_of(c * 128, 128), 128)] = far[...]
    f2[pl.ds(pl.multiple_of((1 - c) * 128, 128), 128)] = far_o[...]
    ft[pl.ds(pl.multiple_of(c * BLOCK, BLOCK), BLOCK)] = near[...]
    ft[pl.ds(pl.multiple_of((1 - c) * BLOCK, BLOCK), BLOCK)] = near_o[...]
    scale, bias = par_ref[0], par_ref[1]
    end = END
    zf, inv2 = normalise(f2[...], himg[...])
    zf2[...] = zf
    z2[...] = zf.astype(BF16)
    zf, inv_t = normalise(ft[...], htxt[...])
    zft[...] = zf
    zt[...] = zf.astype(BF16)
    ft2[...] = dot(pick[...], f2[...], NT).astype(BF16)
    ftt[...] = dot(pick[...], ft[...], NT).astype(BF16)
    score(z2[...], zown[HI], scale, bias, None, gt2, kept2)
    score(zi[...], zt[...], scale, bias, None, gts, kept)
    loss = loss_near[...] + softplus_rows(kept[pl.ds(pl.multiple_of(c * BLOCK, BLOCK), BLOCK)])
    loss_out[...] = jnp.transpose(jnp.broadcast_to(loss, (BLOCK, 128)))[:1]
    loss_far[...] = jnp.transpose(jnp.broadcast_to(softplus_rows(kept2[...]), (BLOCK, 128)))[:1]
    du_i[end] = backnorm(dot(gt2[...], zown[HI]), zf2[...], inv2)
    du_t[2 * BLOCK : 3 * BLOCK] = du3[...]
    du_t[3 * BLOCK :] = backnorm(g4[...] + dot(gt2[...], z2[...], TN), zown[HI].astype(F32) + lzown[HI], invown[HI])
    pair = slice(0, 2 * BLOCK)
    du_i[pair] = backnorm(dq[...] + dot(gts[...], zt[...]), zi[...].astype(F32) + lzi[...], inv[...])
    du_t[pair] = backnorm(dot(gts[...], zi[...], TN), zft[...], inv_t)
    for first in range(0, WIDTH, 256):
        cols = slice(first, min(first + 256, WIDTH))
        g_i = dot(fti[...], du_i[: 2 * BLOCK, cols]) + dot(ft2[...], du_i[end, cols])
        g_t = dot(ftt[...], du_t[: 2 * BLOCK, cols]) + dot(ft34[...], du_t[2 * BLOCK :, cols])
        wide = g_i.shape[1]
        both = jnp.concatenate([g_i.reshape(8, 72, wide), g_t.reshape(8, 72, wide)], axis=1)
        out[:, cols] = both.reshape(WIDTH, wide).astype(BF16)


def half_kernel(got, out, total, parts):
    acc = got[0:144].astype(F32)
    for j in range(1, 8):
        acc += got[144 * j : 144 * (j + 1)].astype(F32)
    total[...] = acc
    parts[...] = jnp.zeros_like(parts)
    for m in range(16):
        for l in range(9):
            parts[88 * m + 9 * l : 88 * m + 9 * l + 9] = total[9 * m : 9 * m + 9, 128 * l : 128 * (l + 1)]
    out[...] = parts[...].astype(BF16)


def last_kernel(core_ref, got, loss, loss_far, out, loss_out, total):
    values = got[...].astype(F32)
    acc = values[:88]
    for j in range(1, 16):
        acc += values[88 * j : 88 * (j + 1)]
    total[...] = acc
    for l in range(9):
        out[:, 128 * l : 128 * (l + 1)] = total[9 * l : 9 * l + 9]
    loss_out[...] = loss[...] + jnp.where(core_ref[0] == 0, loss_far[...], 0.0)


def call(kernel, out_shape, scratch, flops, spaces, limit=24 * MIB):
    vmem = pl.BlockSpec(memory_space=pltpu.VMEM)
    spec = {"s": pl.BlockSpec(memory_space=pltpu.SMEM), "v": vmem, "h": pl.BlockSpec(memory_space=pltpu.HBM)}
    return pl.pallas_call(
        kernel,
        out_shape=out_shape,
        in_specs=[spec[k] for k in spaces],
        out_specs=jax.tree.map(lambda _: vmem, out_shape),
        scratch_shapes=scratch,
        compiler_params=pltpu.CompilerParams(vmem_limit_bytes=limit),
        cost_estimate=pl.CostEstimate(flops=flops, bytes_accessed=8 * MIB, transcendentals=0),
    )


def shapes(dtype, *dims):
    return [jax.ShapeDtypeStruct(d, dtype) for d in dims]


def scratches(dtype, *dims):
    return [pltpu.VMEM(d, dtype) for d in dims]


def local(images, texts, img_head, txt_head, log_scale, bias):
    img, txt = images[0], texts[0]
    c = lax.axis_index("c")
    first = c == 0
    core = jnp.reshape(c, (1,)).astype(jnp.int32)
    params = jnp.stack([jnp.exp(log_scale), bias])

    def swap(a):
        return lax.ppermute(a, AXES, core_swap())

    near = lax.ppermute(txt, AXES, chip_shift(1))
    other_img = swap(img)
    far = lax.ppermute(jnp.where(first, img[:128], other_img[128:]), AXES, chip_shift(-2))
    other_txt = swap(txt)

    one, two, three = (BLOCK, WIDTH), (2 * BLOCK, WIDTH), (3 * BLOCK, WIDTH)
    square, head, column = (WIDTH, WIDTH), (576, WIDTH), (BLOCK, 1)
    kept = call(
        early_kernel,
        shapes(BF16, two, two) + shapes(F32, (512, 1)) + shapes(BF16, (576, 512), head, two, two)
        + shapes(F32, (512, 1)) + shapes(BF16, (576, 512)),
        scratches(BF16, square, square, two, two) + [pltpu.SemaphoreType.DMA((6,))],
        2 * 6 * 340_000_000, "ssvvvvhh", 44 * MIB,
    )(core, params, img, txt, other_img, other_txt, img_head, txt_head)

    near, far, *kept = lax.optimization_barrier((near, far, *kept))
    near_o, far_o = swap(near), swap(far)
    zi, zt, lzt, invt = kept[0], kept[5], kept[6], kept[7]
    own = call(
        own_kernel,
        shapes(F32, column, two, one) + shapes(BF16, one), scratches(BF16, (512, 512)) + scratches(F32, (512, 512)),
        2 * 2 * 340_000_000, "ssvvvv", 12 * MIB,
    )(core, params, zi, zt, lzt, invt)
    term, loss, loss_far = call(
        late_kernel,
        shapes(BF16, square) + shapes(F32, (1, BLOCK), (1, BLOCK)),
        scratches(BF16, two, one, two) + scratches(F32, two) + scratches(BF16, one) + scratches(F32, one)
        + scratches(BF16, (512, 512), (BLOCK, BLOCK)) + scratches(F32, (512, 512), (BLOCK, BLOCK))
        + scratches(BF16, three, (4 * BLOCK, WIDTH), (576, 512), (576, BLOCK)),
        2 * 10 * 340_000_000, "ss" + "v" * 19,
    )(core, params, near, near_o, far, far_o, img_head, txt_head, *kept, *own)

    loss_far = lax.ppermute(loss_far, AXES, chip_shift(2))
    got = lax.all_to_all(term, AXES, 0, 0, axis_index_groups=first_groups(), tiled=True)
    (half,) = call(
        half_kernel, shapes(BF16, (1408, 128)), scratches(F32, (144, WIDTH), (1408, 128)), 10_000_000, "v",
    )(got)
    got = lax.all_to_all(half, AXES, 0, 0, axis_index_groups=second_groups(), tiled=True)
    shares, loss = call(
        last_kernel, shapes(F32, (9, WIDTH), (1, BLOCK)), scratches(F32, (88, 128)), 1_000_000, "svvv",
    )(core, got, loss, loss_far)
    return (loss, shares)


def solution(mesh):
    inner = Mesh(mesh.devices.reshape(NZ, NY, 2, 2, 2), AXES)
    dp = ("z", "y", "xh", "c")
    placed = (P("xl", dp, None), P("xl", dp, None), P(), P(), P(), P())
    return jax.shard_map(
        local,
        mesh=inner,
        in_specs=placed,
        out_specs=(P("xl", dp), P(AXES, None)),
        check_vma=False,
    )
```

```python
import jax
import jax.numpy as jnp
from jax import lax
from jax.experimental import pallas as pl
from jax.experimental.pallas import tpu as pltpu
from jax.sharding import Mesh, PartitionSpec as P

AXES = ("z", "y", "xh", "c", "xl")
NZ, NY, NX = 8, 4, 4
BLOCK = 256
WIDTH = 1152
MIB = 1 << 20
BF16, F32 = jnp.bfloat16, jnp.float32


def place(i):
    return i // 32, (i // 8) % 4, ((i // 4) % 2) * 2 + i % 2, (i // 2) % 2


def index(z, y, x, c):
    return (((z * NY + y) * 2 + x // 2) * 2 + c) * 2 + x % 2


def chip_shift(by):
    pairs = []
    for i in range(256):
        z, y, x, c = place(i)
        q = (((z * NY + y) * 2 + x // 2) + by) % 64
        pairs.append((i, index(q // 8, (q // 2) % 4, (q % 2) * 2 + x % 2, c)))
    return pairs


def core_swap():
    return [(i, index(*place(i)[:3], 1 - place(i)[3])) for i in range(256)]


def grouped(key, order):
    found = {}
    for i in range(256):
        found.setdefault(key(*place(i)), []).append(i)
    return [sorted(v, key=lambda i: order(*place(i))) for v in found.values()]


def first_groups():
    return grouped(
        lambda z, y, x, c: (c, y, z // 2) if c == 0 else (c, x, ((z + 1) % NZ) // 2),
        lambda z, y, x, c: (z % 2, x if c == 0 else y),
    )


def second_groups():
    return grouped(
        lambda z, y, x, c: (c, x if c == 0 else y, z % 2),
        lambda z, y, x, c: (z // 2, y if c == 0 else x),
    )


def head_rows(c):
    r = lax.broadcasted_iota(jnp.int32, (576, 1), 0)

    def digit(r, size, count):
        d = sum((r >= size * k).astype(jnp.int32) for k in range(1, count))
        return d, r - size * d

    zl, r = digit(r, 288, 2)
    a, r = digit(r, 72, 4)
    zh, r = digit(r, 36, 2)
    b, r = digit(r, 9, 4)
    x, y = jnp.where(c == 0, a, b), jnp.where(c == 0, b, a)
    device = (((2 * zh + zl) * 4 + y) * 2 + (x >> 1)) * 4 + c * 2 + (x & 1)
    return 9 * device + r


def dot(a, b, contract=((1,), (0,))):
    return lax.dot_general(a, b, (contract, ((), ())), preferred_element_type=jnp.float32)


NT = ((1,), (1,))
TN = ((0,), (0,))


def normalise(feats, head):
    u = dot(feats, head)
    inv = lax.rsqrt(jnp.sum(u * u, axis=-1, keepdims=True) + 1e-06)
    return u * inv, inv


def rest(zf):
    return (zf - zf.astype(BF16).astype(F32)).astype(BF16)


def backnorm(grad, zfull, inv):
    return (inv * (grad - zfull * jnp.sum(grad * zfull, axis=-1, keepdims=True))).astype(BF16)


def score(query, keys, scale, bias, diagonal, gt_ref, kept):
    logits = scale * dot(query, keys, NT) + bias
    if diagonal is not None:
        row = lax.broadcasted_iota(jnp.int32, logits.shape, 0)
        col = lax.broadcasted_iota(jnp.int32, logits.shape, 1)
        own = col == row + diagonal
        logits = jnp.where(own, -logits, logits)
    kept[...] = logits
    e = jnp.exp(-jnp.abs(logits))
    sig = jnp.where(logits >= 0, 1.0, e) / (1.0 + e)
    if diagonal is not None:
        sig = jnp.where(own, -sig, sig)
    gt_ref[...] = (scale * sig / BLOCK).astype(BF16)


def softplus_rows(x):
    return jnp.sum(jnp.maximum(x, 0.0) + jnp.log1p(jnp.exp(-jnp.abs(x))), axis=1, keepdims=True)


LO, HI, END = (slice(k * BLOCK, (k + 1) * BLOCK) for k in range(3))


def early_kernel(
    core_ref, par_ref, img, txt, oimg, otxt, himg_hbm, htxt_hbm,
    zi, lzi, inv, fti, pick, zt, lzt, invt, ft34,
    himg, htxt, fimg, ftxt, sems,
):
    c = core_ref[0]
    mine, other = pl.multiple_of(c * BLOCK, BLOCK), pl.multiple_of((1 - c) * BLOCK, BLOCK)
    copies = [
        pltpu.make_async_copy(src, dst, sems.at[k])
        for k, (src, dst) in enumerate((
            (img, fimg.at[pl.ds(mine, BLOCK)]), (oimg, fimg.at[pl.ds(other, BLOCK)]), (himg_hbm, himg),
            (txt, ftxt.at[pl.ds(mine, BLOCK)]), (otxt, ftxt.at[pl.ds(other, BLOCK)]), (htxt_hbm, htxt),
        ))
    ]
    for copy in copies:
        copy.start()
    pick[...] = (lax.broadcasted_iota(jnp.int32, (576, WIDTH), 1) == head_rows(c)).astype(BF16)
    for f, ft, head, z, lz, i, waits in (
        (fimg, fti, himg, zi, lzi, inv, copies[:3]), (ftxt, ft34, htxt, zt, lzt, invt, copies[3:]),
    ):
        for copy in waits:
            copy.wait()
        ft[...] = dot(pick[...], f[...], NT).astype(BF16)
        zf, i[...] = normalise(f[...], head[...])
        lz[...] = rest(zf)
        z[...] = zf.astype(BF16)


def own_kernel(core_ref, par_ref, zi, zt, lzt, invt, loss, dq, g4, du3, gts, kept):
    c = core_ref[0]
    scale, bias = par_ref[0], par_ref[1]
    kept[LO, HI] = jnp.full((BLOCK, BLOCK), -1e30, F32)
    score(zi[LO], zt[LO], scale, bias, 0, gts.at[LO, LO], kept.at[LO, LO])
    score(zi[HI], zt[...], scale, bias, BLOCK, gts.at[HI, :], kept.at[HI, :])
    loss[...] = softplus_rows(kept[pl.ds(pl.multiple_of(c * BLOCK, BLOCK), BLOCK)])
    dq[LO] = dot(gts[LO, LO], zt[LO])
    dq[HI] = dot(gts[HI, :], zt[...])
    du3[...] = backnorm(dot(gts[:, LO], zi[...], TN), zt[LO].astype(F32) + lzt[LO], invt[LO])
    g4[...] = dot(gts[HI, HI], zi[HI], TN)


def late_kernel(
    core_ref, par_ref, near, near_o, far, far_o,
    himg, htxt, zi, lzi, inv, fti, pick, zown, lzown, invown, ft34, loss_near, dq, g4, du3,
    out, loss_out, loss_far,
    ft, f2, zt, zft, z2, zf2, gts, gt2, kept, kept2, du_i, du_t, ftt, ft2,
):
    c = core_ref[0]
    f2[pl.ds(pl.multiple_of(c * 128, 128), 128)] = far[...]
    f2[pl.ds(pl.multiple_of((1 - c) * 128, 128), 128)] = far_o[...]
    ft[pl.ds(pl.multiple_of(c * BLOCK, BLOCK), BLOCK)] = near[...]
    ft[pl.ds(pl.multiple_of((1 - c) * BLOCK, BLOCK), BLOCK)] = near_o[...]
    scale, bias = par_ref[0], par_ref[1]
    end = END
    zf, inv2 = normalise(f2[...], himg[...])
    zf2[...] = zf
    z2[...] = zf.astype(BF16)
    zf, inv_t = normalise(ft[...], htxt[...])
    zft[...] = zf
    zt[...] = zf.astype(BF16)
    score(z2[...], zown[HI], scale, bias, None, gt2, kept2)
    score(zi[...], zt[...], scale, bias, None, gts, kept)
    ft2[...] = dot(pick[...], f2[...], NT).astype(BF16)
    ftt[...] = dot(pick[...], ft[...], NT).astype(BF16)
    du_i[end] = backnorm(dot(gt2[...], zown[HI]), zf2[...], inv2)
    du_t[2 * BLOCK : 3 * BLOCK] = du3[...]
    du_t[3 * BLOCK :] = backnorm(g4[...] + dot(gt2[...], z2[...], TN), zown[HI].astype(F32) + lzown[HI], invown[HI])
    pair = slice(0, 2 * BLOCK)
    du_i[pair] = backnorm(dq[...] + dot(gts[...], zt[...]), zi[...].astype(F32) + lzi[...], inv[...])
    du_t[pair] = backnorm(dot(gts[...], zi[...], TN), zft[...], inv_t)
    loss = loss_near[...] + softplus_rows(kept[pl.ds(pl.multiple_of(c * BLOCK, BLOCK), BLOCK)])
    loss_out[...] = jnp.transpose(jnp.broadcast_to(loss, (BLOCK, 128)))[:1]
    loss_far[...] = jnp.transpose(jnp.broadcast_to(softplus_rows(kept2[...]), (BLOCK, 128)))[:1]
    for first in range(0, WIDTH, 256):
        cols = slice(first, min(first + 256, WIDTH))
        g_i = dot(fti[...], du_i[: 2 * BLOCK, cols]) + dot(ft2[...], du_i[end, cols])
        g_t = dot(ftt[...], du_t[: 2 * BLOCK, cols]) + dot(ft34[...], du_t[2 * BLOCK :, cols])
        wide = g_i.shape[1]
        both = jnp.concatenate([g_i.reshape(8, 72, wide), g_t.reshape(8, 72, wide)], axis=1)
        out[:, cols] = both.reshape(WIDTH, wide).astype(BF16)


def half_kernel(got, out, total, parts):
    acc = got[0:144].astype(F32)
    for j in range(1, 8):
        acc += got[144 * j : 144 * (j + 1)].astype(F32)
    total[...] = acc
    parts[...] = jnp.zeros_like(parts)
    for m in range(16):
        for l in range(9):
            parts[88 * m + 9 * l : 88 * m + 9 * l + 9] = total[9 * m : 9 * m + 9, 128 * l : 128 * (l + 1)]
    out[...] = parts[...].astype(BF16)


def last_kernel(core_ref, got, loss, loss_far, out, loss_out, total):
    values = got[...].astype(F32)
    acc = values[:88]
    for j in range(1, 16):
        acc += values[88 * j : 88 * (j + 1)]
    total[...] = acc
    for l in range(9):
        out[:, 128 * l : 128 * (l + 1)] = total[9 * l : 9 * l + 9]
    loss_out[...] = loss[...] + jnp.where(core_ref[0] == 0, loss_far[...], 0.0)


def call(kernel, out_shape, scratch, flops, spaces, limit=24 * MIB):
    vmem = pl.BlockSpec(memory_space=pltpu.VMEM)
    spec = {"s": pl.BlockSpec(memory_space=pltpu.SMEM), "v": vmem, "h": pl.BlockSpec(memory_space=pltpu.HBM)}
    return pl.pallas_call(
        kernel,
        out_shape=out_shape,
        in_specs=[spec[k] for k in spaces],
        out_specs=jax.tree.map(lambda _: vmem, out_shape),
        scratch_shapes=scratch,
        compiler_params=pltpu.CompilerParams(vmem_limit_bytes=limit),
        cost_estimate=pl.CostEstimate(flops=flops, bytes_accessed=8 * MIB, transcendentals=0),
    )


def shapes(dtype, *dims):
    return [jax.ShapeDtypeStruct(d, dtype) for d in dims]


def scratches(dtype, *dims):
    return [pltpu.VMEM(d, dtype) for d in dims]


def local(images, texts, img_head, txt_head, log_scale, bias):
    img, txt = images[0], texts[0]
    c = lax.axis_index("c")
    first = c == 0
    core = jnp.reshape(c, (1,)).astype(jnp.int32)
    params = jnp.stack([jnp.exp(log_scale), bias])

    def swap(a):
        return lax.ppermute(a, AXES, core_swap())

    near = lax.ppermute(txt, AXES, chip_shift(1))
    other_img = swap(img)
    far = lax.ppermute(jnp.where(first, img[:128], other_img[128:]), AXES, chip_shift(-2))
    other_txt = swap(txt)

    one, two, three = (BLOCK, WIDTH), (2 * BLOCK, WIDTH), (3 * BLOCK, WIDTH)
    square, head, column = (WIDTH, WIDTH), (576, WIDTH), (BLOCK, 1)
    kept = call(
        early_kernel,
        shapes(BF16, two, two) + shapes(F32, (512, 1)) + shapes(BF16, (576, 512), head, two, two)
        + shapes(F32, (512, 1)) + shapes(BF16, (576, 512)),
        scratches(BF16, square, square, two, two) + [pltpu.SemaphoreType.DMA((6,))],
        2 * 6 * 340_000_000, "ssvvvvhh", 44 * MIB,
    )(core, params, img, txt, other_img, other_txt, img_head, txt_head)

    near, far, *kept = lax.optimization_barrier((near, far, *kept))
    near_o, far_o = swap(near), swap(far)
    zi, zt, lzt, invt = kept[0], kept[5], kept[6], kept[7]
    own = call(
        own_kernel,
        shapes(F32, column, two, one) + shapes(BF16, one), scratches(BF16, (512, 512)) + scratches(F32, (512, 512)),
        2 * 2 * 340_000_000, "ssvvvv", 12 * MIB,
    )(core, params, zi, zt, lzt, invt)
    term, loss, loss_far = call(
        late_kernel,
        shapes(BF16, square) + shapes(F32, (1, BLOCK), (1, BLOCK)),
        scratches(BF16, two, one, two) + scratches(F32, two) + scratches(BF16, one) + scratches(F32, one)
        + scratches(BF16, (512, 512), (BLOCK, BLOCK)) + scratches(F32, (512, 512), (BLOCK, BLOCK))
        + scratches(BF16, three, (4 * BLOCK, WIDTH), (576, 512), (576, BLOCK)),
        2 * 10 * 340_000_000, "ss" + "v" * 19,
    )(core, params, near, near_o, far, far_o, img_head, txt_head, *kept, *own)

    loss_far = lax.ppermute(loss_far, AXES, chip_shift(2))
    got = lax.all_to_all(term, AXES, 0, 0, axis_index_groups=first_groups(), tiled=True)
    (half,) = call(
        half_kernel, shapes(BF16, (1408, 128)), scratches(F32, (144, WIDTH), (1408, 128)), 10_000_000, "v",
    )(got)
    got = lax.all_to_all(half, AXES, 0, 0, axis_index_groups=second_groups(), tiled=True)
    shares, loss = call(
        last_kernel, shapes(F32, (9, WIDTH), (1, BLOCK)), scratches(F32, (88, 128)), 1_000_000, "svvv",
    )(core, got, loss, loss_far)
    return (loss, shares)


def solution(mesh):
    inner = Mesh(mesh.devices.reshape(NZ, NY, 2, 2, 2), AXES)
    dp = ("z", "y", "xh", "c")
    placed = (P("xl", dp, None), P("xl", dp, None), P(), P(), P(), P())
    return jax.shard_map(
        local,
        mesh=inner,
        in_specs=placed,
        out_specs=(P("xl", dp), P(AXES, None)),
        check_vma=False,
    )
```
